512 devices in a mesh: dp: 8 (over y_hi, x), fsdp: 64 (over y_lo, z, core).
Axes of the slice: x: 4, y: 8 (y_hi: 2, y_lo: 4; y = y_hi * 4 + y_lo), z: 8, core: 2. Of those that a mesh axis runs over, the one named last changes fastest.
Arguments:
- activations: bfloat16 [131072, 8192], P(('dp', 'fsdp')), may hold values from -24 to 24
- value_weight: bfloat16 [8192, 128], P('fsdp'), may hold values from -0.0625 to 0.0625
- sensitivity: bfloat16 [131072, 128], P(('dp', 'fsdp')), may hold values from -6 to 6
- policy_logp: float32 [131072], P(('dp', 'fsdp')), may hold values from -0.7 to -0.3
- reference_logp: float32 [131072], P(('dp', 'fsdp')), may hold values from -0.7 to -0.3
- prompt_len: int32 [16], replicated, may hold values from 512 to 2047
Outputs:
- projected: bfloat16 [131072, 128], P(('dp', 'fsdp'))
- weight_grad: float32 [8192, 128], P('fsdp')
- margins: float32 [16], replicated
- loss: float32 [], replicated
The draws below stay inside these ranges and needn't reach their ends.
Inputs may be any that keep to these rules, and one draw needn't show every extreme that they name: `prompt_len`: shared by the chosen and the rejected sequence of the pair.
All inputs are finite; a program needn't handle non-finite values.
Results may differ from the reference program's by a relative error of at most 0.0029.
Values may be sent and summed in bfloat16 or wider, within the bound.
No kernel may reach another device: no remote copies, remote signals or barrier semaphores. Data moves between devices by JAX's collectives and lax.ppermute only.
A program may use at most 64 MiB of HBM per device.

```python
import jax
import jax.numpy as jnp
from jax import lax

D = 8192
HEAD = 128
SEQ = 4096
TOKENS = 131072
PAIRS = 16


def touch_ends(array, own_key, low, high):
    spot = [jax.random.randint(jax.random.fold_in(own_key, axis), (), 0, length) for axis, length in enumerate(array.shape)]
    longest = array.shape.index(max(array.shape))
    neighbour = spot[:longest] + [(spot[longest] + 1) % array.shape[longest]] + spot[longest + 1:]
    return array.at[tuple(spot)].set(low).at[tuple(neighbour)].set(high)


def raised(values, stream_key, source, target, shards_of, factor):
    owner, partner = [(jnp.arange(values.shape[axis_at]) // (values.shape[axis_at] // shards_of)).reshape([-1 if axis == axis_at else 1 for axis in range(values.ndim)]) for axis_at in (source, target)]
    chosen = jax.random.permutation(stream_key, shards_of)[partner]
    strong = (owner == chosen) | (owner == (partner + shards_of // 2) % shards_of)
    return jnp.where(strong, factor * values, values)


def block_levels(own_key, shape, split, low, largest):
    factor_of = 1.0
    for dim, parts in split:
        steps = jax.random.uniform(jax.random.fold_in(jax.random.fold_in(own_key, 6), dim), (parts,), jnp.float32, low / len(split), largest / len(split))
        factor_of = factor_of * jnp.repeat(jnp.exp(steps), shape[dim] // parts).reshape((-1,) + (1,) * (len(shape) - 1 - dim))
    return factor_of


def bell_draw(stream_key, dims, deviation, reach, shards=(), kind=jnp.bfloat16):
    array = jax.random.normal(stream_key, dims, jnp.float32) * deviation
    if len(shards) > 0:
        array = block_levels(stream_key, dims, shards, -0.22, 0.18) * array
    return jnp.clip(array, min=-reach, max=reach).astype(kind)


def noise_with(own_key, extent, width, limit, pieces, heavy, held_as=jnp.bfloat16):
    drawn = width * jax.random.normal(own_key, extent, jnp.float32)
    if pieces:
        drawn = drawn * block_levels(own_key, extent, pieces, -0.22, 0.18)
    return jnp.clip(raised(drawn, jax.random.fold_in(own_key, 3), *heavy), -limit, limit).astype(held_as)


def setup_inputs(seed: int = 0) -> dict:
    key_of = jax.random.split(jax.random.key(seed), 7)
    activations = noise_with(key_of[0], (TOKENS, D), 1.0, 24.0, ((0, 512),), (0, 1, 512, 6.0))
    value_weight = bell_draw(key_of[1], (D, HEAD), D ** -0.5, 0.0625, ((0, 64),))
    sensitivity = bell_draw(key_of[2], (TOKENS, HEAD), 1.0, 6.0, ((0, 512),))
    policy_logp = jnp.clip(-0.7 + 0.39999998 * jax.random.uniform(key_of[3], (TOKENS,), jnp.float32) ** block_levels(key_of[3], (TOKENS,), ((0, 512),), -0.2, 0.2), -0.7, -0.3)
    reference_logp = jnp.clip(-0.7 + 0.39999998 * jax.random.uniform(key_of[4], (TOKENS,), jnp.float32) ** block_levels(key_of[4], (TOKENS,), ((0, 512),), -0.2, 0.2), -0.7, -0.3)
    prompt_len = touch_ends(jax.random.randint(key_of[5], (PAIRS,), SEQ // 8, SEQ // 2), jax.random.fold_in(key_of[5], 1), SEQ // 8, (SEQ // 2) - 1).astype(jnp.int32)
    return {"activations": activations, "value_weight": value_weight, "sensitivity": sensitivity, "policy_logp": policy_logp, "reference_logp": reference_logp, "prompt_len": prompt_len}


BETA = 0.1


def reference(activations, value_weight, sensitivity, policy_logp, reference_logp, prompt_len):
    projected = jnp.dot(activations, value_weight, preferred_element_type=jnp.float32).astype(jnp.bfloat16)
    pair_count = prompt_len.shape[0]
    seq_count = 2 * pair_count
    offset = jnp.arange(SEQ, dtype=jnp.int32)
    prompt_seq = jnp.repeat(prompt_len, 2)
    mask = offset[None, :] >= prompt_seq[:, None]
    difference = (policy_logp - reference_logp).reshape(seq_count, SEQ)
    totals = jnp.sum(jnp.where(mask, difference, jnp.float32(0.0)), axis=1)
    margins = BETA * (totals[0::2] - totals[1::2])
    loss = jnp.mean(jax.nn.softplus(-margins))
    pair_scale = -BETA * jax.nn.sigmoid(-margins) / pair_count
    seq_scale = jnp.stack([pair_scale, -pair_scale], axis=1).reshape(seq_count)
    token_scale = jnp.where(mask, seq_scale[:, None], jnp.float32(0.0)).reshape(-1)
    cotangent = (token_scale[:, None] * sensitivity.astype(jnp.float32)).astype(jnp.bfloat16)
    weight_grad = lax.dot_general(activations, cotangent, (((0,), (0,)), ((), ())), preferred_element_type=jnp.float32)
    return projected, weight_grad, margins, loss
```

```python
import jax
import jax.numpy as jnp
from jax import lax
from jax.sharding import Mesh, PartitionSpec as P

SEQ = 4096
BETA = 0.1
HEAD = 128
EXTRA = 16

SIZES = (("yh", 2), ("x", 4), ("yp", 2), ("yq", 2), ("z", 8), ("c", 2))
NAMES = tuple(name for name, _ in SIZES)
DP = ("yh", "x")
FSDP = ("yp", "yq", "z", "c")
SWAP = ((0, 1), (1, 0))


def pieces(value):
    high = lax.reduce_precision(value, 8, 7)
    rest = value - high
    middle = lax.reduce_precision(rest, 8, 7)
    low = lax.reduce_precision(rest - middle, 8, 7)
    return jnp.stack([high, middle, low]).astype(jnp.bfloat16)


def packed(value):
    rows = jnp.concatenate([pieces(value), jnp.zeros((EXTRA - 3,), jnp.bfloat16)])
    return jnp.broadcast_to(rows[:, None], (EXTRA, HEAD))


def unpacked(rows):
    return jnp.sum(rows[..., :3, 0].astype(jnp.float32), axis=-1)


def pick(index, first, second):
    return jnp.where(index == 0, first, second)


def body(activations, value_weight, sensitivity, policy_logp, reference_logp, prompt_len):
    row_count, width = activations.shape
    pair_count = prompt_len.shape[0]
    yh, x, yp, yq, z, c = (lax.axis_index(name) for name in NAMES)
    xs, zs = 4, 8
    blocks = width // HEAD // 2

    pair = (yh * xs + x) * 2 + yp
    prompt_here = lax.dynamic_index_in_dim(prompt_len, pair, keepdims=False)
    ramp = jnp.arange(row_count, dtype=jnp.int32)
    mask_own = (z * 2 + c) * row_count + ramp >= prompt_here
    mask_other = (z * 2 + 1 - c) * row_count + ramp >= prompt_here
    part = jnp.sum(jnp.where(mask_own, policy_logp - reference_logp, jnp.float32(0.0)))

    sens_and_part = jnp.concatenate([sensitivity, packed(part)])
    other = lax.ppermute(sens_and_part, "c", SWAP)
    sens_other = other[:row_count]
    part_chip = part + unpacked(other[row_count:])
    by_core = activations.reshape(row_count, blocks, 2, HEAD)
    even, odd = by_core[:, :, 0], by_core[:, :, 1]
    act_own = pick(c, even, odd).reshape(row_count, width // 2)
    act_other = lax.ppermute(pick(c, odd, even).reshape(row_count, width // 2), "c", SWAP)

    block = jnp.concatenate([value_weight, packed(part_chip)])
    height = block.shape[0]
    near = lax.all_to_all(
        jnp.broadcast_to(block[None], (2 * zs, height, HEAD)).reshape(-1, HEAD), ("yq", "z"), 0, 0, tiled=True
    ).reshape(2 * zs, height, HEAD)
    totals = jnp.sum(unpacked(near[:, HEAD:]).reshape(2, zs), axis=1)
    margin = BETA * (totals[0] - totals[1])

    outside = [(y, (y + 1) % 8 if y % 2 else (y - 1) % 8) for y in range(8)]
    far = lax.ppermute(near, ("yh", "yp", "yq"), outside)
    far_totals = jnp.sum(unpacked(far[:, HEAD:]).reshape(2, zs), axis=1)
    far_margin = BETA * (far_totals[0] - far_totals[1])

    pair_scale = -BETA * jax.nn.sigmoid(-margin) / pair_count
    scale = pick(yq, pair_scale, -pair_scale)

    def cotangent(mask, sens):
        token_scale = jnp.where(mask, scale, jnp.float32(0.0))
        return (token_scale[:, None] * sens.astype(jnp.float32)).astype(jnp.bfloat16)

    def term(act, mask, sens):
        return lax.dot_general(
            act, cotangent(mask, sens), (((0,), (0,)), ((), ())), preferred_element_type=jnp.float32
        )

    grad = term(act_own, mask_own, sensitivity) + term(act_other, mask_other, sens_other)
    rows = HEAD // xs
    grad = grad.reshape(blocks, xs, rows, HEAD)

    def chunk(index):
        return lax.dynamic_index_in_dim(grad, index % xs, axis=1, keepdims=False)

    reduced = chunk(x)
    for step in (2, 1, 3):
        sent = lax.ppermute(
            chunk(x + step).astype(jnp.bfloat16), "x", [(i, (i + step) % xs) for i in range(xs)]
        )
        reduced = reduced + sent.astype(jnp.float32)
    terms = lax.all_to_all(
        reduced.astype(jnp.bfloat16).reshape(blocks * rows, HEAD), ("yp", "yq", "z"), 0, 0, tiled=True
    ).reshape(blocks, rows, HEAD)
    reduced = jnp.sum(terms.astype(jnp.float32), axis=0)

    near_w, far_w = near[:, :HEAD].reshape(-1, HEAD), far[:, :HEAD].reshape(-1, HEAD)
    weight = jnp.concatenate([pick(yp, near_w, far_w), pick(yp, far_w, near_w)])
    half_own = jnp.dot(act_own, weight, preferred_element_type=jnp.float32)
    half_other = jnp.dot(act_other, weight, preferred_element_type=jnp.float32)
    projected = (half_own + lax.ppermute(half_other, "c", SWAP)).astype(jnp.bfloat16)

    tail = jnp.concatenate([
        jnp.broadcast_to(margin, (1, HEAD)),
        jnp.broadcast_to(far_margin, (1, HEAD)),
        jnp.zeros((6, HEAD), jnp.float32),
    ])
    share = jnp.concatenate([reduced, tail])
    high = share.shape[0]
    shares = lax.all_to_all(
        jnp.broadcast_to(share[None], (2 * xs, high, HEAD)).reshape(-1, HEAD), DP, 0, 0, tiled=True
    ).reshape(2, xs, high, HEAD)
    weight_grad = (shares[0, :, :rows] + shares[1, :, :rows]).reshape(HEAD, HEAD)
    near_m = shares[:, :, rows, 0]
    far_m = shares[:, :, rows + 1, 0]
    far_m = jnp.where(yp == yq, far_m[::-1], far_m)
    margins = jnp.stack([pick(yp, near_m, far_m), pick(yp, far_m, near_m)], axis=-1).reshape(pair_count)
    loss = jnp.mean(jax.nn.softplus(-margins))
    return projected, weight_grad, margins, loss


def solution(mesh):
    devices = mesh.devices.reshape(tuple(size for _, size in SIZES))
    return jax.shard_map(
        body,
        mesh=Mesh(devices, NAMES),
        in_specs=(
            P(DP + FSDP, None),
            P(FSDP, None),
            P(DP + FSDP, None),
            P(DP + FSDP),
            P(DP + FSDP),
            P(),
        ),
        out_specs=(P(DP + FSDP, None), P(FSDP, None), P(), P()),
        check_vma=False,
    )
```

```python
import functools

import jax
import jax.numpy as jnp
from jax import lax
from jax.experimental import pallas as pl
from jax.experimental.pallas import tpu as pltpu
from jax.sharding import Mesh, PartitionSpec as P

SEQ = 4096
BETA = 0.1
HEAD = 128
EXTRA = 16
PAIRS = 16
ROWS = 256
WIDTH = 8192
HALF = WIDTH // 2
BLOCKS = HALF // HEAD
XS, ZS = 4, 8
SHARE = HEAD // XS
NEAR = 2 * ZS

SIZES = (("yh", 2), ("x", XS), ("yp", 2), ("yq", 2), ("z", ZS), ("c", 2))
NAMES = tuple(name for name, _ in SIZES)
DP = ("yh", "x")
FSDP = ("yp", "yq", "z", "c")
SWAP = ((0, 1), (1, 0))
F32, BF16 = jnp.float32, jnp.bfloat16

VMEM = pl.BlockSpec(memory_space=pltpu.VMEM)
SMEM = pl.BlockSpec(memory_space=pltpu.SMEM)


def local(kernel, out_shape, in_specs, *args, flops=0, moved=0, megabytes=8, **more):
    return pl.pallas_call(
        kernel,
        out_shape=out_shape,
        in_specs=in_specs,
        compiler_params=pltpu.CompilerParams(vmem_limit_bytes=megabytes << 20),
        cost_estimate=pl.CostEstimate(flops=flops, bytes_accessed=moved, transcendentals=0),
        **more,
    )(*args)


def shape(dims, kind):
    return jax.ShapeDtypeStruct(dims, kind)


def prompt_of(prompt_ref):
    pair = (lax.axis_index("yh") * XS + lax.axis_index("x")) * 2 + lax.axis_index("yp")
    return prompt_ref[pair]


def offset_of(core):
    return (lax.axis_index("z") * 2 + core) * ROWS


def total_kernel(prompt_ref, policy_ref, reference_ref, out_ref):
    at = lax.broadcasted_iota(jnp.int32, (2, HEAD), 0) * HEAD + lax.broadcasted_iota(jnp.int32, (2, HEAD), 1)
    mask = offset_of(lax.axis_index("c")) + at >= prompt_of(prompt_ref)
    part = jnp.sum(jnp.where(mask, policy_ref[...] - reference_ref[...], 0.0))
    out_ref[...] = jnp.full((8, HEAD), part, F32)


def pack_kernel(weight_ref, own_ref, other_ref, out_ref):
    part = own_ref[0:1] + other_ref[0:1]
    high = part.astype(BF16).astype(F32)
    middle = (part - high).astype(BF16).astype(F32)
    low = (part - high) - middle
    row = lax.broadcasted_iota(jnp.int32, (EXTRA, HEAD), 0)
    tile = jnp.where(row == 0, high, jnp.where(row == 1, middle, jnp.where(row == 2, low, 0.0))).astype(BF16)
    for chip in range(NEAR):
        out_ref[chip, :HEAD] = weight_ref[...]
        out_ref[chip, HEAD:] = tile


def split_kernel(act_ref, sens_ref, own_ref, send_ref):
    def move(parity):
        for block in range(BLOCKS):
            to = slice(block * HEAD, (block + 1) * HEAD)
            mine, theirs = (2 * block + parity) * HEAD, (2 * block + 1 - parity) * HEAD
            own_ref[:, to] = act_ref[:, mine : mine + HEAD]
            send_ref[:, to] = act_ref[:, theirs : theirs + HEAD]

    core = lax.axis_index("c")
    pl.when(core == 0)(lambda: move(0))
    pl.when(core == 1)(lambda: move(1))
    send_ref[:, HALF:] = sens_ref[...]


def margin_of(tiles):
    terms = tiles[:, 0:3].astype(F32)
    by_chip = jnp.sum(terms, axis=1)
    chosen = jnp.sum(by_chip[:ZS], axis=0, keepdims=True)
    rejected = jnp.sum(by_chip[ZS:], axis=0, keepdims=True)
    return BETA * (chosen - rejected)


def grad_kernel(prompt_ref, near_ref, own_ref, other_ref, sens_ref, keep_ref, one_ref, two_ref, three_ref, grad_ref):
    margin = margin_of(near_ref[...])
    pair_scale = -BETA * (1.0 / (1.0 + jnp.exp(margin))) / PAIRS
    scale = jnp.where(lax.axis_index("yq") == 0, pair_scale, -pair_scale)
    prompt = prompt_of(prompt_ref)
    core = lax.axis_index("c")
    token = lax.broadcasted_iota(jnp.int32, (ROWS, HEAD), 0)

    def cotangent(sens, index):
        token_scale = jnp.where(offset_of(index) + token >= prompt, scale, 0.0)
        return (token_scale * sens.astype(F32)).astype(BF16).astype(F32).T.astype(BF16)

    mine = cotangent(sens_ref[...], core)
    theirs = cotangent(other_ref[:, HALF:], 1 - core)
    x = lax.axis_index("x")
    step = 512
    for start in range(0, HALF, step):
        to = slice(start, start + step)
        grad_ref[...] = jnp.dot(mine, own_ref[:, to], preferred_element_type=F32) + jnp.dot(
            theirs, other_ref[:, to], preferred_element_type=F32
        )
        def rows(distance):
            return grad_ref[pl.ds(pl.multiple_of(lax.rem(x + distance, XS) * SHARE, SHARE), SHARE), :]
        keep_ref[:, to] = rows(0)
        for distance, ref in ((1, one_ref), (2, two_ref), (3, three_ref)):
            ref[:, to] = rows(distance).astype(BF16)


def add_kernel(keep_ref, one_ref, two_ref, three_ref, out_ref):
    for block in range(BLOCKS):
        at = slice(block * HEAD, (block + 1) * HEAD)
        total = keep_ref[:, at]
        for ref in (one_ref, two_ref, three_ref):
            total = total + ref[:, at].astype(F32)
        out_ref[block] = total.astype(BF16)


def project_kernel(near_ref, far_ref, own_ref, other_ref, mine_ref, theirs_ref):
    yp = lax.axis_index("yp")
    mine = jnp.zeros((ROWS, HEAD), F32)
    theirs = jnp.zeros((ROWS, HEAD), F32)
    for ref, index in ((near_ref, yp), (far_ref, 1 - yp)):
        for chip in range(0, NEAR, 2):
            weight = jnp.concatenate([ref[chip, :HEAD], ref[chip + 1, :HEAD]])
            at = pl.ds(pl.multiple_of(index * (HALF // 2) + chip * HEAD, HEAD), 2 * HEAD)
            mine += jnp.dot(own_ref[:, at], weight, preferred_element_type=F32)
            theirs += jnp.dot(other_ref[:, at], weight, preferred_element_type=F32)
    mine_ref[...] = mine
    theirs_ref[...] = theirs


def join_kernel(terms_ref, near_ref, far_ref, out_ref):
    total = jnp.sum(terms_ref[...].astype(F32), axis=0)
    row = lax.broadcasted_iota(jnp.int32, (8, HEAD), 0)
    tail = jnp.where(row == 0, margin_of(near_ref[...]), margin_of(far_ref[...]))
    for replica in range(2 * XS):
        out_ref[replica, :SHARE] = total
        out_ref[replica, SHARE:] = tail


def last_kernel(shares_ref, grad_ref, margins_ref, loss_ref):
    parts = [shares_ref[x, :SHARE] + shares_ref[XS + x, :SHARE] for x in range(XS)]
    grad_ref[...] = jnp.concatenate(parts).T
    yp, yq = lax.axis_index("yp"), lax.axis_index("yq")
    lane = lax.broadcasted_iota(jnp.int32, (1, HEAD), 1)
    margins = jnp.zeros((1, HEAD), F32)
    for yh in range(2):
        for x in range(XS):
            near = shares_ref[yh * XS + x, SHARE : SHARE + 1]
            flipped = shares_ref[(1 - yh) * XS + x, SHARE + 1 : SHARE + 2]
            straight = shares_ref[yh * XS + x, SHARE + 1 : SHARE + 2]
            far = jnp.where(yp == yq, flipped, straight)
            pair = (yh * XS + x) * 2
            margins = jnp.where(lane == pair + yp, near, margins)
            margins = jnp.where(lane == pair + 1 - yp, far, margins)
    margins_ref[...] = margins[:, :PAIRS]
    losses = jnp.maximum(-margins, 0.0) + jnp.log1p(jnp.exp(-jnp.abs(margins)))
    loss_ref[0, 0] = jnp.sum(jnp.where(lane < PAIRS, losses, 0.0)) / PAIRS


def body(activations, value_weight, sensitivity, policy_logp, reference_logp, prompt_len):
    part = local(
        total_kernel,
        shape((8, HEAD), F32),
        [SMEM, VMEM, VMEM],
        prompt_len, policy_logp.reshape(2, HEAD), reference_logp.reshape(2, HEAD),
        moved=4096,
    )
    part_other = lax.ppermute(part, "c", SWAP)
    height = HEAD + EXTRA
    packed = local(
        pack_kernel,
        shape((NEAR, height, HEAD), BF16),
        [VMEM] * 3,
        value_weight, part, part_other,
        moved=600 << 10,
    )
    near = lax.all_to_all(packed.reshape(-1, HEAD), ("yq", "z"), 0, 0, tiled=True).reshape(NEAR, height, HEAD)
    outside = [(y, (y + 1) % 8 if y % 2 else (y - 1) % 8) for y in range(8)]
    far = lax.ppermute(near, ("yh", "yp", "yq"), outside)

    strip = ROWS // 4
    own, send = local(
        split_kernel,
        (shape((ROWS, HALF), BF16), shape((ROWS, HALF + HEAD), BF16)),
        [pl.BlockSpec((strip, WIDTH), lambda i: (i, 0)), pl.BlockSpec((strip, HEAD), lambda i: (i, 0))],
        activations, sensitivity,
        moved=8 << 20,
        grid=(4,),
        out_specs=(
            pl.BlockSpec((strip, HALF), lambda i: (i, 0)),
            pl.BlockSpec((strip, HALF + HEAD), lambda i: (i, 0)),
        ),
    )
    other = lax.ppermute(send, "c", SWAP)

    tile = pl.BlockSpec((NEAR, EXTRA, HEAD), lambda i: (0, HEAD // EXTRA, 0))
    whole = lambda dims: pl.BlockSpec(dims, lambda i: (0,) * len(dims))
    keep, one, two, three = local(
        grad_kernel,
        (shape((SHARE, HALF), F32),) + (shape((SHARE, HALF), BF16),) * 3,
        [SMEM, tile, whole((ROWS, HALF)), whole((ROWS, HALF + HEAD)), whole((ROWS, HEAD))],
        prompt_len, near, own, other, sensitivity,
        flops=2 * 2 * ROWS * HALF * HEAD, moved=6 << 20, megabytes=24,
        grid=(1,),
        out_specs=(whole((SHARE, HALF)),) * 4,
        scratch_shapes=[pltpu.VMEM((HEAD, 512), F32)],
    )
    sent = [
        lax.ppermute(chunk, "x", [(i, (i + step) % XS) for i in range(XS)])
        for step, chunk in ((1, one), (2, two), (3, three))
    ]
    summed = local(add_kernel, shape((BLOCKS, SHARE, HEAD), BF16), [VMEM] * 4, keep, *sent, moved=2 << 20)
    terms = lax.all_to_all(summed.reshape(-1, HEAD), ("yp", "yq", "z"), 0, 0, tiled=True)

    mine, theirs = local(
        project_kernel,
        (shape((ROWS, HEAD), F32),) * 2,
        [VMEM] * 4,
        near, far, own, other,
        flops=2 * 2 * ROWS * HALF * HEAD, moved=6 << 20, megabytes=24,
    )
    projected = (mine + lax.ppermute(theirs, "c", SWAP)).astype(BF16)

    high = SHARE + 8
    joined = local(
        join_kernel,
        shape((2 * XS, high, HEAD), F32),
        [whole((BLOCKS, SHARE, HEAD)), tile, tile],
        terms.reshape(BLOCKS, SHARE, HEAD), near, far,
        moved=1 << 20,
        grid=(1,),
        out_specs=whole((2 * XS, high, HEAD)),
    )
    shares = lax.all_to_all(joined.reshape(-1, HEAD), DP, 0, 0, tiled=True).reshape(2 * XS, high, HEAD)
    weight_grad, margins, loss = local(
        last_kernel,
        (shape((HEAD, HEAD), F32), shape((1, PAIRS), F32), shape((1, 1), F32)),
        [VMEM],
        shares,
        moved=300 << 10,
        out_specs=(VMEM, VMEM, SMEM),
    )
    return projected, weight_grad, margins.reshape(PAIRS), loss.reshape(())


def solution(mesh):
    devices = mesh.devices.reshape(tuple(size for _, size in SIZES))
    return jax.shard_map(
        body,
        mesh=Mesh(devices, NAMES),
        in_specs=(
            P(DP + FSDP, None),
            P(FSDP, None),
            P(DP + FSDP, None),
            P(DP + FSDP),
            P(DP + FSDP),
            P(),
        ),
        out_specs=(P(DP + FSDP, None), P(FSDP, None), P(), P()),
        check_vma=False,
    )
```

```python
import functools

import jax
import jax.numpy as jnp
from jax import lax
from jax.experimental import pallas as pl
from jax.experimental.pallas import tpu as pltpu
from jax.sharding import Mesh, PartitionSpec as P

SEQ = 4096
BETA = 0.1
HEAD = 128
EXTRA = 16
PAIRS = 16
ROWS = 256
WIDTH = 8192
HALF = WIDTH // 2
BLOCKS = HALF // HEAD
XS, ZS = 4, 8
SHARE = HEAD // XS
NEAR = 2 * ZS

SIZES = (("yh", 2), ("x", XS), ("yp", 2), ("yq", 2), ("z", ZS), ("c", 2))
NAMES = tuple(name for name, _ in SIZES)
DP = ("yh", "x")
FSDP = ("yp", "yq", "z", "c")
SWAP = ((0, 1), (1, 0))
F32, BF16 = jnp.float32, jnp.bfloat16

VMEM = pl.BlockSpec(memory_space=pltpu.VMEM)
ANY = pl.BlockSpec(memory_space=pl.ANY)
SMEM = pl.BlockSpec(memory_space=pltpu.SMEM)


def local(kernel, out_shape, in_specs, *args, flops=0, moved=0, megabytes=8, **more):
    return pl.pallas_call(
        kernel,
        out_shape=out_shape,
        in_specs=in_specs,
        compiler_params=pltpu.CompilerParams(vmem_limit_bytes=megabytes << 20),
        cost_estimate=pl.CostEstimate(flops=flops, bytes_accessed=moved, transcendentals=0),
        **more,
    )(*args)


def shape(dims, kind):
    return jax.ShapeDtypeStruct(dims, kind)


def prompt_of(prompt_ref):
    pair = (lax.axis_index("yh") * XS + lax.axis_index("x")) * 2 + lax.axis_index("yp")
    return prompt_ref[pair]


def offset_of(core):
    return (lax.axis_index("z") * 2 + core) * ROWS


def total_kernel(prompt_ref, policy_ref, reference_ref, out_ref):
    at = lax.broadcasted_iota(jnp.int32, (2, HEAD), 0) * HEAD + lax.broadcasted_iota(jnp.int32, (2, HEAD), 1)
    mask = offset_of(lax.axis_index("c")) + at >= prompt_of(prompt_ref)
    part = jnp.sum(jnp.where(mask, policy_ref[...] - reference_ref[...], 0.0))
    out_ref[...] = jnp.full(out_ref.shape, part, F32)


def pack_kernel(weight_ref, parts_ref, one_ref, two_ref, three_ref, out_ref, *same_refs):
    del one_ref, two_ref, three_ref, same_refs
    row = lax.broadcasted_iota(jnp.int32, (EXTRA, HEAD), 0)
    tile = jnp.zeros((EXTRA, HEAD), F32)
    for x in range(XS):
        part = parts_ref[2 * x, 0:1] + parts_ref[2 * x + 1, 0:1]
        high = part.astype(BF16).astype(F32)
        middle = (part - high).astype(BF16).astype(F32)
        for at, value in enumerate((high, middle, (part - high) - middle)):
            tile = jnp.where(row == 3 * x + at, value, tile)
    for chip in range(NEAR):
        out_ref[chip, :HEAD] = weight_ref[...]
        out_ref[chip, HEAD:] = tile.astype(BF16)


def columns_of(act_ref, out_ref, index):
    def move(parity):
        for block in range(BLOCKS):
            start = (2 * block + parity) * HEAD
            out_ref[:, block * HEAD : (block + 1) * HEAD] = act_ref[:, start : start + HEAD]

    pl.when(index == 0)(lambda: move(0))
    pl.when(index == 1)(lambda: move(1))


def send_kernel(act_ref, sens_ref, out_ref):
    columns_of(act_ref, out_ref, 1 - lax.axis_index("c"))
    out_ref[:, HALF:] = sens_ref[...]


def own_kernel(act_ref, after_ref, out_ref):
    del after_ref
    columns_of(act_ref, out_ref, lax.axis_index("c"))


def margins_of(tiles):
    tiles = tiles.astype(F32)
    chosen, rejected = jnp.sum(tiles[:ZS], axis=0), jnp.sum(tiles[ZS:], axis=0)
    return [
        BETA * (jnp.sum(chosen[at : at + 3], axis=0, keepdims=True) - jnp.sum(rejected[at : at + 3], axis=0, keepdims=True))
        for at in range(0, 3 * XS, 3)
    ]


def pick_x(rows, x):
    picked = rows[0]
    for at in range(1, XS):
        picked = jnp.where(x == at, rows[at], picked)
    return picked


def grad_kernel(prompt_ref, own_ref, other_ref, sens_ref, keep_ref, one_ref, two_ref, three_ref, grad_ref):
    prompt = prompt_of(prompt_ref)
    core = lax.axis_index("c")
    token = lax.broadcasted_iota(jnp.int32, (ROWS, HEAD), 0)

    def masked(sens, index):
        return jnp.where(offset_of(index) + token >= prompt, sens.astype(F32), 0.0).T.astype(BF16)

    mine = masked(sens_ref[...], core)
    theirs = masked(other_ref[:, HALF:], 1 - core)
    x = lax.axis_index("x")
    step = 512
    for start in range(0, HALF, step):
        to = slice(start, start + step)
        grad_ref[...] = jnp.dot(mine, own_ref[:, to], preferred_element_type=F32) + jnp.dot(
            theirs, other_ref[:, to], preferred_element_type=F32
        )
        def rows(distance):
            return grad_ref[pl.ds(pl.multiple_of(lax.rem(x + distance, XS) * SHARE, SHARE), SHARE), :]
        keep_ref[:, to] = rows(0)
        for distance, ref in ((1, one_ref), (2, two_ref), (3, three_ref)):
            ref[:, to] = rows(distance).astype(BF16)


def add_kernel(near_ref, keep_ref, one_ref, two_ref, three_ref, out_ref):
    x = lax.axis_index("x")
    sign = jnp.where(lax.axis_index("yq") == 0, -BETA / PAIRS, BETA / PAIRS)
    scales = [sign / (1.0 + jnp.exp(margin)) for margin in margins_of(near_ref[...])]
    refs = (keep_ref, one_ref, two_ref, three_ref)
    scale = [pick_x(scales, lax.rem(x + XS - distance, XS)) for distance in range(XS)]
    for block in range(BLOCKS):
        at = slice(block * HEAD, (block + 1) * HEAD)
        total = scale[0] * keep_ref[:, at]
        for distance in range(1, XS):
            total = total + scale[distance] * refs[distance][:, at].astype(F32)
        out_ref[block] = total.astype(BF16)


def project_kernel(near_ref, far_ref, own_ref, other_ref, mine_ref, theirs_ref):
    yp = lax.axis_index("yp")
    mine = jnp.zeros((ROWS, HEAD), F32)
    theirs = jnp.zeros((ROWS, HEAD), F32)
    for ref, index in ((near_ref, yp), (far_ref, 1 - yp)):
        for chip in range(0, NEAR, 2):
            weight = jnp.concatenate([ref[chip, :HEAD], ref[chip + 1, :HEAD]])
            at = pl.ds(pl.multiple_of(index * (HALF // 2) + chip * HEAD, HEAD), 2 * HEAD)
            mine += jnp.dot(own_ref[:, at], weight, preferred_element_type=F32)
            theirs += jnp.dot(other_ref[:, at], weight, preferred_element_type=F32)
    mine_ref[...] = mine
    theirs_ref[...] = theirs


def join_kernel(terms_ref, near_ref, far_ref, out_ref):
    total = jnp.sum(terms_ref[...].astype(F32), axis=0)
    row = lax.broadcasted_iota(jnp.int32, (8, HEAD), 0)
    x = lax.axis_index("x")
    tail = jnp.where(row == 0, pick_x(margins_of(near_ref[...]), x), pick_x(margins_of(far_ref[...]), x))
    for replica in range(2 * XS):
        out_ref[replica, :SHARE] = total
        out_ref[replica, SHARE:] = tail


def last_kernel(shares_ref, grad_ref, margins_ref, loss_ref):
    parts = [shares_ref[x, :SHARE] + shares_ref[XS + x, :SHARE] for x in range(XS)]
    grad_ref[...] = jnp.concatenate(parts).T
    yp, yq = lax.axis_index("yp"), lax.axis_index("yq")
    lane = lax.broadcasted_iota(jnp.int32, (1, HEAD), 1)
    margins = jnp.zeros((1, HEAD), F32)
    for yh in range(2):
        for x in range(XS):
            near = shares_ref[yh * XS + x, SHARE : SHARE + 1]
            flipped = shares_ref[(1 - yh) * XS + x, SHARE + 1 : SHARE + 2]
            straight = shares_ref[yh * XS + x, SHARE + 1 : SHARE + 2]
            far = jnp.where(yp == yq, flipped, straight)
            pair = (yh * XS + x) * 2
            margins = jnp.where(lane == pair + yp, near, margins)
            margins = jnp.where(lane == pair + 1 - yp, far, margins)
    margins_ref[...] = margins[:, :PAIRS]
    losses = jnp.maximum(-margins, 0.0) + jnp.log1p(jnp.exp(-jnp.abs(margins)))
    loss_ref[0, 0] = jnp.sum(jnp.where(lane < PAIRS, losses, 0.0)) / PAIRS


def body(activations, value_weight, sensitivity, policy_logp, reference_logp, prompt_len):
    part = local(
        total_kernel,
        shape((2 * XS, 8, HEAD), F32),
        [SMEM, VMEM, VMEM],
        prompt_len, policy_logp.reshape(2, HEAD), reference_logp.reshape(2, HEAD),
        moved=40 << 10,
    )
    parts = lax.all_to_all(part.reshape(-1, HEAD), ("x", "c"), 0, 0, tiled=True).reshape(2 * XS, 8, HEAD)
    strip = ROWS // 4
    rows_of = lambda width: pl.BlockSpec((strip, width), lambda i: (i, 0))
    send = local(
        send_kernel,
        shape((ROWS, HALF + HEAD), BF16),
        [rows_of(WIDTH), rows_of(HEAD)],
        activations, sensitivity,
        moved=6 << 20,
        grid=(4,),
        out_specs=rows_of(HALF + HEAD),
    )
    own = local(
        own_kernel,
        shape((ROWS, HALF), BF16),
        [rows_of(WIDTH), ANY],
        activations, part,
        moved=6 << 20,
        grid=(4,),
        out_specs=rows_of(HALF),
    )
    other = lax.ppermute(send, "c", SWAP)

    tile = pl.BlockSpec((NEAR, EXTRA, HEAD), lambda i: (0, HEAD // EXTRA, 0))
    whole = lambda dims: pl.BlockSpec(dims, lambda i: (0,) * len(dims))
    keep, one, two, three = local(
        grad_kernel,
        (shape((SHARE, HALF), F32),) + (shape((SHARE, HALF), BF16),) * 3,
        [SMEM, whole((ROWS, HALF)), whole((ROWS, HALF + HEAD)), whole((ROWS, HEAD))],
        prompt_len, own, other, sensitivity,
        flops=2 * 2 * ROWS * HALF * HEAD, moved=6 << 20, megabytes=24,
        grid=(1,),
        out_specs=(whole((SHARE, HALF)),) * 4,
        scratch_shapes=[pltpu.VMEM((HEAD, 512), F32)],
    )
    height = HEAD + EXTRA
    packed, one, two, three = local(
        pack_kernel,
        (shape((NEAR, height, HEAD), BF16),) + (shape((SHARE, HALF), BF16),) * 3,
        [VMEM] * 2 + [ANY] * 3,
        value_weight, parts, one, two, three,
        moved=600 << 10,
        out_specs=(VMEM, ANY, ANY, ANY),
        input_output_aliases={2: 1, 3: 2, 4: 3},
    )
    near = lax.all_to_all(packed.reshape(-1, HEAD), ("yq", "z"), 0, 0, tiled=True).reshape(NEAR, height, HEAD)
    outside = [(y, (y + 1) % 8 if y % 2 else (y - 1) % 8) for y in range(8)]
    far = lax.ppermute(near, ("yh", "yp", "yq"), outside)

    sent = [
        lax.ppermute(chunk, "x", [(i, (i + step) % XS) for i in range(XS)])
        for step, chunk in ((1, one), (2, two), (3, three))
    ]
    summed = local(
        add_kernel,
        shape((BLOCKS, SHARE, HEAD), BF16),
        [tile, whole((SHARE, HALF))] + [whole((SHARE, HALF))] * 3,
        near, keep, *sent,
        moved=2 << 20,
        grid=(1,),
        out_specs=whole((BLOCKS, SHARE, HEAD)),
    )
    terms = lax.all_to_all(summed.reshape(-1, HEAD), ("yp", "yq", "z"), 0, 0, tiled=True)

    mine, theirs = local(
        project_kernel,
        (shape((ROWS, HEAD), F32),) * 2,
        [VMEM] * 4,
        near, far, own, other,
        flops=2 * 2 * ROWS * HALF * HEAD, moved=6 << 20, megabytes=24,
    )
    projected = (mine + lax.ppermute(theirs, "c", SWAP)).astype(BF16)

    high = SHARE + 8
    joined = local(
        join_kernel,
        shape((2 * XS, high, HEAD), F32),
        [whole((BLOCKS, SHARE, HEAD)), tile, tile],
        terms.reshape(BLOCKS, SHARE, HEAD), near, far,
        moved=1 << 20,
        grid=(1,),
        out_specs=whole((2 * XS, high, HEAD)),
    )
    shares = lax.all_to_all(joined.reshape(-1, HEAD), DP, 0, 0, tiled=True).reshape(2 * XS, high, HEAD)
    weight_grad, margins, loss = local(
        last_kernel,
        (shape((HEAD, HEAD), F32), shape((1, PAIRS), F32), shape((1, 1), F32)),
        [VMEM],
        shares,
        moved=300 << 10,
        out_specs=(VMEM, VMEM, SMEM),
    )
    return projected, weight_grad, margins.reshape(PAIRS), loss.reshape(())


def solution(mesh):
    devices = mesh.devices.reshape(tuple(size for _, size in SIZES))
    return jax.shard_map(
        body,
        mesh=Mesh(devices, NAMES),
        in_specs=(
            P(DP + FSDP, None),
            P(FSDP, None),
            P(DP + FSDP, None),
            P(DP + FSDP),
            P(DP + FSDP),
            P(),
        ),
        out_specs=(P(DP + FSDP, None), P(FSDP, None), P(), P()),
        check_vma=False,
    )
```

```python
import functools

import jax
import jax.numpy as jnp
from jax import lax
from jax.experimental import pallas as pl
from jax.experimental.pallas import tpu as pltpu
from jax.sharding import Mesh, PartitionSpec as P

SEQ = 4096
BETA = 0.1
HEAD = 128
EXTRA = 16
PAIRS = 16
ROWS = 256
WIDTH = 8192
HALF = WIDTH // 2
BLOCKS = HALF // HEAD
XS, ZS = 4, 8
SHARE = HEAD // XS
LEAST = SHARE // 2
NEAR = 2 * ZS

SIZES = (("yh", 2), ("x", XS), ("yp", 2), ("yq", 2), ("z", ZS), ("c", 2))
NAMES = tuple(name for name, _ in SIZES)
DP = ("yh", "x")
FSDP = ("yp", "yq", "z", "c")
SWAP = ((0, 1), (1, 0))
F32, BF16 = jnp.float32, jnp.bfloat16

VMEM = pl.BlockSpec(memory_space=pltpu.VMEM)
SMEM = pl.BlockSpec(memory_space=pltpu.SMEM)


def local(kernel, out_shape, in_specs, *args, flops=0, moved=0, megabytes=8, **more):
    return pl.pallas_call(
        kernel,
        out_shape=out_shape,
        in_specs=in_specs,
        compiler_params=pltpu.CompilerParams(vmem_limit_bytes=megabytes << 20),
        cost_estimate=pl.CostEstimate(flops=flops, bytes_accessed=moved, transcendentals=0),
        **more,
    )(*args)


def shape(dims, kind):
    return jax.ShapeDtypeStruct(dims, kind)


def prompt_of(prompt_ref):
    pair = (lax.axis_index("yh") * XS + lax.axis_index("x")) * 2 + lax.axis_index("yp")
    return prompt_ref[pair]


def offset_of(core):
    return (lax.axis_index("z") * 2 + core) * ROWS


def total_kernel(prompt_ref, policy_ref, reference_ref, out_ref):
    at = lax.broadcasted_iota(jnp.int32, (2, HEAD), 0) * HEAD + lax.broadcasted_iota(jnp.int32, (2, HEAD), 1)
    mask = offset_of(lax.axis_index("c")) + at >= prompt_of(prompt_ref)
    part = jnp.sum(jnp.where(mask, policy_ref[...] - reference_ref[...], 0.0))
    out_ref[...] = jnp.full((8, HEAD), part, F32)


def pack_kernel(weight_ref, own_ref, other_ref, out_ref):
    part = own_ref[0:1] + other_ref[0:1]
    high = part.astype(BF16).astype(F32)
    middle = (part - high).astype(BF16).astype(F32)
    low = (part - high) - middle
    row = lax.broadcasted_iota(jnp.int32, (EXTRA, HEAD), 0)
    tile = jnp.where(row == 0, high, jnp.where(row == 1, middle, jnp.where(row == 2, low, 0.0))).astype(BF16)
    for chip in range(NEAR):
        out_ref[chip, :HEAD] = weight_ref[...]
        out_ref[chip, HEAD:] = tile


def split_kernel(act_ref, sens_ref, own_ref, send_ref):
    def move(parity):
        for block in range(BLOCKS):
            to = slice(block * HEAD, (block + 1) * HEAD)
            mine, theirs = (2 * block + parity) * HEAD, (2 * block + 1 - parity) * HEAD
            own_ref[:, to] = act_ref[:, mine : mine + HEAD]
            send_ref[:, to] = act_ref[:, theirs : theirs + HEAD]

    core = lax.axis_index("c")
    pl.when(core == 0)(lambda: move(0))
    pl.when(core == 1)(lambda: move(1))
    send_ref[:, HALF:] = sens_ref[...]


def margin_of(tiles):
    terms = tiles[:, 0:3].astype(F32)
    by_chip = jnp.sum(terms, axis=1)
    chosen = jnp.sum(by_chip[:ZS], axis=0, keepdims=True)
    rejected = jnp.sum(by_chip[ZS:], axis=0, keepdims=True)
    return BETA * (chosen - rejected)


def grad_kernel(prompt_ref, near_ref, own_ref, other_ref, sens_ref, keep_ref, one_ref, two_ref, three_ref, grad_ref):
    margin = margin_of(near_ref[...])
    pair_scale = -BETA * (1.0 / (1.0 + jnp.exp(margin))) / PAIRS
    scale = jnp.where(lax.axis_index("yq") == 0, pair_scale, -pair_scale)
    prompt = prompt_of(prompt_ref)
    core = lax.axis_index("c")
    token = lax.broadcasted_iota(jnp.int32, (ROWS, HEAD), 0)

    def cotangent(sens, index):
        token_scale = jnp.where(offset_of(index) + token >= prompt, scale, 0.0)
        return (token_scale * sens.astype(F32)).astype(BF16).astype(F32).T.astype(BF16)

    mine = cotangent(sens_ref[...], core)
    theirs = cotangent(other_ref[:, HALF:], 1 - core)
    x = lax.axis_index("x")
    step = 512
    for start in range(0, HALF, step):
        to = slice(start, start + step)
        grad_ref[...] = jnp.dot(mine, own_ref[:, to], preferred_element_type=F32) + jnp.dot(
            theirs, other_ref[:, to], preferred_element_type=F32
        )
        def rows(distance):
            return grad_ref[pl.ds(pl.multiple_of(lax.rem(x + distance, XS) * SHARE, SHARE), SHARE), :]
        keep_ref[:, to] = rows(0)
        for distance, ref in ((1, one_ref), (2, two_ref), (3, three_ref)):
            ref[:, to] = rows(distance).astype(BF16)


def add_kernel(keep_ref, one_ref, two_ref, three_ref, out_ref):
    for block in range(BLOCKS):
        at = slice(block * HEAD, (block + 1) * HEAD)
        total = keep_ref[:, at]
        for ref in (one_ref, two_ref, three_ref):
            total = total + ref[:, at].astype(F32)
        total = total.astype(BF16)
        for yh in range(2):
            out_ref[yh, block] = total[yh * LEAST : (yh + 1) * LEAST]


def project_kernel(near_ref, far_ref, own_ref, other_ref, mine_ref, theirs_ref):
    yp = lax.axis_index("yp")
    mine = jnp.zeros((ROWS, HEAD), F32)
    theirs = jnp.zeros((ROWS, HEAD), F32)
    for ref, index in ((near_ref, yp), (far_ref, 1 - yp)):
        for chip in range(0, NEAR, 2):
            weight = jnp.concatenate([ref[chip, :HEAD], ref[chip + 1, :HEAD]])
            at = pl.ds(pl.multiple_of(index * (HALF // 2) + chip * HEAD, HEAD), 2 * HEAD)
            mine += jnp.dot(own_ref[:, at], weight, preferred_element_type=F32)
            theirs += jnp.dot(other_ref[:, at], weight, preferred_element_type=F32)
    mine_ref[...] = mine
    theirs_ref[...] = theirs


def join_kernel(terms_ref, near_ref, far_ref, out_ref):
    total = jnp.sum(terms_ref[...].astype(F32), axis=0)
    row = lax.broadcasted_iota(jnp.int32, (8, HEAD), 0)
    tail = jnp.where(row == 0, margin_of(near_ref[...]), margin_of(far_ref[...]))
    for replica in range(2 * XS):
        out_ref[replica, :LEAST] = total
        out_ref[replica, LEAST:] = tail


def last_kernel(shares_ref, grad_ref, margins_ref, loss_ref):
    parts = [shares_ref[yh * XS + x, :LEAST] for x in range(XS) for yh in range(2)]
    grad_ref[...] = jnp.concatenate(parts).T
    yp, yq = lax.axis_index("yp"), lax.axis_index("yq")
    lane = lax.broadcasted_iota(jnp.int32, (1, HEAD), 1)
    margins = jnp.zeros((1, HEAD), F32)
    for yh in range(2):
        for x in range(XS):
            near = shares_ref[yh * XS + x, LEAST : LEAST + 1]
            flipped = shares_ref[(1 - yh) * XS + x, LEAST + 1 : LEAST + 2]
            straight = shares_ref[yh * XS + x, LEAST + 1 : LEAST + 2]
            far = jnp.where(yp == yq, flipped, straight)
            pair = (yh * XS + x) * 2
            margins = jnp.where(lane == pair + yp, near, margins)
            margins = jnp.where(lane == pair + 1 - yp, far, margins)
    margins_ref[...] = margins[:, :PAIRS]
    losses = jnp.maximum(-margins, 0.0) + jnp.log1p(jnp.exp(-jnp.abs(margins)))
    loss_ref[0, 0] = jnp.sum(jnp.where(lane < PAIRS, losses, 0.0)) / PAIRS


def body(activations, value_weight, sensitivity, policy_logp, reference_logp, prompt_len):
    part = local(
        total_kernel,
        shape((8, HEAD), F32),
        [SMEM, VMEM, VMEM],
        prompt_len, policy_logp.reshape(2, HEAD), reference_logp.reshape(2, HEAD),
        moved=4096,
    )
    part_other = lax.ppermute(part, "c", SWAP)
    height = HEAD + EXTRA
    packed = local(
        pack_kernel,
        shape((NEAR, height, HEAD), BF16),
        [VMEM] * 3,
        value_weight, part, part_other,
        moved=600 << 10,
    )
    near = lax.all_to_all(packed.reshape(-1, HEAD), ("yq", "z"), 0, 0, tiled=True).reshape(NEAR, height, HEAD)
    outside = [(y, (y + 1) % 8 if y % 2 else (y - 1) % 8) for y in range(8)]
    far = lax.ppermute(near, ("yh", "yp", "yq"), outside)

    strip = ROWS // 4
    own, send = local(
        split_kernel,
        (shape((ROWS, HALF), BF16), shape((ROWS, HALF + HEAD), BF16)),
        [pl.BlockSpec((strip, WIDTH), lambda i: (i, 0)), pl.BlockSpec((strip, HEAD), lambda i: (i, 0))],
        activations, sensitivity,
        moved=8 << 20,
        grid=(4,),
        out_specs=(
            pl.BlockSpec((strip, HALF), lambda i: (i, 0)),
            pl.BlockSpec((strip, HALF + HEAD), lambda i: (i, 0)),
        ),
    )
    other = lax.ppermute(send, "c", SWAP)

    tile = pl.BlockSpec((NEAR, EXTRA, HEAD), lambda i: (0, HEAD // EXTRA, 0))
    whole = lambda dims: pl.BlockSpec(dims, lambda i: (0,) * len(dims))
    keep, one, two, three = local(
        grad_kernel,
        (shape((SHARE, HALF), F32),) + (shape((SHARE, HALF), BF16),) * 3,
        [SMEM, tile, whole((ROWS, HALF)), whole((ROWS, HALF + HEAD)), whole((ROWS, HEAD))],
        prompt_len, near, own, other, sensitivity,
        flops=2 * 2 * ROWS * HALF * HEAD, moved=6 << 20, megabytes=24,
        grid=(1,),
        out_specs=(whole((SHARE, HALF)),) * 4,
        scratch_shapes=[pltpu.VMEM((HEAD, 512), F32)],
    )
    sent = [
        lax.ppermute(chunk, "x", [(i, (i + step) % XS) for i in range(XS)])
        for step, chunk in ((1, one), (2, two), (3, three))
    ]
    summed = local(add_kernel, shape((2, BLOCKS, LEAST, HEAD), BF16), [VMEM] * 4, keep, *sent, moved=2 << 20)
    terms = lax.all_to_all(summed.reshape(-1, HEAD), ("yh", "yp", "yq", "z"), 0, 0, tiled=True)

    mine, theirs = local(
        project_kernel,
        (shape((ROWS, HEAD), F32),) * 2,
        [VMEM] * 4,
        near, far, own, other,
        flops=2 * 2 * ROWS * HALF * HEAD, moved=6 << 20, megabytes=24,
    )
    projected = (mine + lax.ppermute(theirs, "c", SWAP)).astype(BF16)

    high = LEAST + 8
    joined = local(
        join_kernel,
        shape((2 * XS, high, HEAD), F32),
        [whole((2 * BLOCKS, LEAST, HEAD)), tile, tile],
        terms.reshape(2 * BLOCKS, LEAST, HEAD), near, far,
        moved=1 << 20,
        grid=(1,),
        out_specs=whole((2 * XS, high, HEAD)),
    )
    shares = lax.all_to_all(joined.reshape(-1, HEAD), DP, 0, 0, tiled=True).reshape(2 * XS, high, HEAD)
    weight_grad, margins, loss = local(
        last_kernel,
        (shape((HEAD, HEAD), F32), shape((1, PAIRS), F32), shape((1, 1), F32)),
        [VMEM],
        shares,
        moved=300 << 10,
        out_specs=(VMEM, VMEM, SMEM),
    )
    return projected, weight_grad, margins.reshape(PAIRS), loss.reshape(())


def solution(mesh):
    devices = mesh.devices.reshape(tuple(size for _, size in SIZES))
    return jax.shard_map(
        body,
        mesh=Mesh(devices, NAMES),
        in_specs=(
            P(DP + FSDP, None),
            P(FSDP, None),
            P(DP + FSDP, None),
            P(DP + FSDP),
            P(DP + FSDP),
            P(),
        ),
        out_specs=(P(DP + FSDP, None), P(FSDP, None), P(), P()),
        check_vma=False,
    )
```

```python
import functools

import jax
import jax.numpy as jnp
from jax import lax
from jax.experimental import pallas as pl
from jax.experimental.pallas import tpu as pltpu
from jax.sharding import Mesh, PartitionSpec as P

SEQ = 4096
BETA = 0.1
HEAD = 128
EXTRA = 16
PAIRS = 16
ROWS = 256
WIDTH = 8192
HALF = WIDTH // 2
BLOCKS = HALF // HEAD
XS, ZS = 4, 8
SHARE = HEAD // XS
NEAR = 2 * ZS

SIZES = (("yh", 2), ("x", XS), ("yp", 2), ("yq", 2), ("z", ZS), ("c", 2))
NAMES = tuple(name for name, _ in SIZES)
DP = ("yh", "x")
FSDP = ("yp", "yq", "z", "c")
SWAP = ((0, 1), (1, 0))
F32, BF16 = jnp.float32, jnp.bfloat16

VMEM = pl.BlockSpec(memory_space=pltpu.VMEM)
ANY = pl.BlockSpec(memory_space=pl.ANY)
SMEM = pl.BlockSpec(memory_space=pltpu.SMEM)


def local(kernel, out_shape, in_specs, *args, flops=0, moved=0, megabytes=8, **more):
    return pl.pallas_call(
        kernel,
        out_shape=out_shape,
        in_specs=in_specs,
        compiler_params=pltpu.CompilerParams(vmem_limit_bytes=megabytes << 20),
        cost_estimate=pl.CostEstimate(flops=flops, bytes_accessed=moved, transcendentals=0),
        **more,
    )(*args)


def shape(dims, kind):
    return jax.ShapeDtypeStruct(dims, kind)


def prompt_of(prompt_ref):
    pair = (lax.axis_index("yh") * XS + lax.axis_index("x")) * 2 + lax.axis_index("yp")
    return prompt_ref[pair]


def offset_of(core):
    return (lax.axis_index("z") * 2 + core) * ROWS


def total_kernel(prompt_ref, policy_ref, reference_ref, out_ref):
    at = lax.broadcasted_iota(jnp.int32, (2, HEAD), 0) * HEAD + lax.broadcasted_iota(jnp.int32, (2, HEAD), 1)
    mask = offset_of(lax.axis_index("c")) + at >= prompt_of(prompt_ref)
    part = jnp.sum(jnp.where(mask, policy_ref[...] - reference_ref[...], 0.0))
    out_ref[...] = jnp.full(out_ref.shape, part, F32)


def pack_kernel(weight_ref, parts_ref, one_ref, two_ref, three_ref, out_ref, *same_refs):
    del one_ref, two_ref, three_ref, same_refs
    row = lax.broadcasted_iota(jnp.int32, (EXTRA, HEAD), 0)
    tile = jnp.zeros((EXTRA, HEAD), F32)
    for x in range(XS):
        part = parts_ref[2 * x, 0:1] + parts_ref[2 * x + 1, 0:1]
        high = part.astype(BF16).astype(F32)
        middle = (part - high).astype(BF16).astype(F32)
        for at, value in enumerate((high, middle, (part - high) - middle)):
            tile = jnp.where(row == 3 * x + at, value, tile)
    for chip in range(NEAR):
        out_ref[chip, :HEAD] = weight_ref[...]
        out_ref[chip, HEAD:] = tile.astype(BF16)


def split_kernel(act_ref, sens_ref, own_ref, send_ref):
    def move(parity):
        for block in range(BLOCKS):
            to = slice(block * HEAD, (block + 1) * HEAD)
            mine, theirs = (2 * block + parity) * HEAD, (2 * block + 1 - parity) * HEAD
            own_ref[:, to] = act_ref[:, mine : mine + HEAD]
            send_ref[:, to] = act_ref[:, theirs : theirs + HEAD]

    core = lax.axis_index("c")
    pl.when(core == 0)(lambda: move(0))
    pl.when(core == 1)(lambda: move(1))
    send_ref[:, HALF:] = sens_ref[...]


def margins_of(tiles):
    tiles = tiles.astype(F32)
    chosen, rejected = jnp.sum(tiles[:ZS], axis=0), jnp.sum(tiles[ZS:], axis=0)
    return [
        BETA * (jnp.sum(chosen[at : at + 3], axis=0, keepdims=True) - jnp.sum(rejected[at : at + 3], axis=0, keepdims=True))
        for at in range(0, 3 * XS, 3)
    ]


def pick_x(rows, x):
    picked = rows[0]
    for at in range(1, XS):
        picked = jnp.where(x == at, rows[at], picked)
    return picked


def grad_kernel(prompt_ref, own_ref, other_ref, sens_ref, keep_ref, one_ref, two_ref, three_ref, grad_ref):
    prompt = prompt_of(prompt_ref)
    core = lax.axis_index("c")
    token = lax.broadcasted_iota(jnp.int32, (ROWS, HEAD), 0)

    def masked(sens, index):
        return jnp.where(offset_of(index) + token >= prompt, sens.astype(F32), 0.0).T.astype(BF16)

    mine = masked(sens_ref[...], core)
    theirs = masked(other_ref[:, HALF:], 1 - core)
    x = lax.axis_index("x")
    step = 512
    for start in range(0, HALF, step):
        to = slice(start, start + step)
        grad_ref[...] = jnp.dot(mine, own_ref[:, to], preferred_element_type=F32) + jnp.dot(
            theirs, other_ref[:, to], preferred_element_type=F32
        )
        def rows(distance):
            return grad_ref[pl.ds(pl.multiple_of(lax.rem(x + distance, XS) * SHARE, SHARE), SHARE), :]
        keep_ref[:, to] = rows(0)
        for distance, ref in ((1, one_ref), (2, two_ref), (3, three_ref)):
            ref[:, to] = rows(distance).astype(BF16)


def add_kernel(near_ref, keep_ref, one_ref, two_ref, three_ref, out_ref):
    x = lax.axis_index("x")
    sign = jnp.where(lax.axis_index("yq") == 0, -BETA / PAIRS, BETA / PAIRS)
    scales = [sign / (1.0 + jnp.exp(margin)) for margin in margins_of(near_ref[...])]
    refs = (keep_ref, one_ref, two_ref, three_ref)
    scale = [pick_x(scales, lax.rem(x + XS - distance, XS)) for distance in range(XS)]
    for block in range(BLOCKS):
        at = slice(block * HEAD, (block + 1) * HEAD)
        total = scale[0] * keep_ref[:, at]
        for distance in range(1, XS):
            total = total + scale[distance] * refs[distance][:, at].astype(F32)
        out_ref[block] = total.astype(BF16)


def project_kernel(near_ref, far_ref, own_ref, other_ref, mine_ref, theirs_ref):
    yp = lax.axis_index("yp")
    mine = jnp.zeros((ROWS, HEAD), F32)
    theirs = jnp.zeros((ROWS, HEAD), F32)
    for ref, index in ((near_ref, yp), (far_ref, 1 - yp)):
        for chip in range(0, NEAR, 2):
            weight = jnp.concatenate([ref[chip, :HEAD], ref[chip + 1, :HEAD]])
            at = pl.ds(pl.multiple_of(index * (HALF // 2) + chip * HEAD, HEAD), 2 * HEAD)
            mine += jnp.dot(own_ref[:, at], weight, preferred_element_type=F32)
            theirs += jnp.dot(other_ref[:, at], weight, preferred_element_type=F32)
    mine_ref[...] = mine
    theirs_ref[...] = theirs


def join_kernel(terms_ref, near_ref, far_ref, out_ref):
    total = jnp.sum(terms_ref[...].astype(F32), axis=0)
    row = lax.broadcasted_iota(jnp.int32, (8, HEAD), 0)
    x = lax.axis_index("x")
    tail = jnp.where(row == 0, pick_x(margins_of(near_ref[...]), x), pick_x(margins_of(far_ref[...]), x))
    for replica in range(2 * XS):
        out_ref[replica, :SHARE] = total
        out_ref[replica, SHARE:] = tail


def last_kernel(shares_ref, grad_ref, margins_ref, loss_ref):
    parts = [shares_ref[x, :SHARE] + shares_ref[XS + x, :SHARE] for x in range(XS)]
    grad_ref[...] = jnp.concatenate(parts).T
    yp, yq = lax.axis_index("yp"), lax.axis_index("yq")
    lane = lax.broadcasted_iota(jnp.int32, (1, HEAD), 1)
    margins = jnp.zeros((1, HEAD), F32)
    for yh in range(2):
        for x in range(XS):
            near = shares_ref[yh * XS + x, SHARE : SHARE + 1]
            flipped = shares_ref[(1 - yh) * XS + x, SHARE + 1 : SHARE + 2]
            straight = shares_ref[yh * XS + x, SHARE + 1 : SHARE + 2]
            far = jnp.where(yp == yq, flipped, straight)
            pair = (yh * XS + x) * 2
            margins = jnp.where(lane == pair + yp, near, margins)
            margins = jnp.where(lane == pair + 1 - yp, far, margins)
    margins_ref[...] = margins[:, :PAIRS]
    losses = jnp.maximum(-margins, 0.0) + jnp.log1p(jnp.exp(-jnp.abs(margins)))
    loss_ref[0, 0] = jnp.sum(jnp.where(lane < PAIRS, losses, 0.0)) / PAIRS


def body(activations, value_weight, sensitivity, policy_logp, reference_logp, prompt_len):
    part = local(
        total_kernel,
        shape((2 * XS, 8, HEAD), F32),
        [SMEM, VMEM, VMEM],
        prompt_len, policy_logp.reshape(2, HEAD), reference_logp.reshape(2, HEAD),
        moved=40 << 10,
    )
    parts = lax.all_to_all(part.reshape(-1, HEAD), ("x", "c"), 0, 0, tiled=True).reshape(2 * XS, 8, HEAD)
    strip = ROWS // 4
    own, send = local(
        split_kernel,
        (shape((ROWS, HALF), BF16), shape((ROWS, HALF + HEAD), BF16)),
        [pl.BlockSpec((strip, WIDTH), lambda i: (i, 0)), pl.BlockSpec((strip, HEAD), lambda i: (i, 0))],
        activations, sensitivity,
        moved=8 << 20,
        grid=(4,),
        out_specs=(
            pl.BlockSpec((strip, HALF), lambda i: (i, 0)),
            pl.BlockSpec((strip, HALF + HEAD), lambda i: (i, 0)),
        ),
    )
    other = lax.ppermute(send, "c", SWAP)

    tile = pl.BlockSpec((NEAR, EXTRA, HEAD), lambda i: (0, HEAD // EXTRA, 0))
    whole = lambda dims: pl.BlockSpec(dims, lambda i: (0,) * len(dims))
    keep, one, two, three = local(
        grad_kernel,
        (shape((SHARE, HALF), F32),) + (shape((SHARE, HALF), BF16),) * 3,
        [SMEM, whole((ROWS, HALF)), whole((ROWS, HALF + HEAD)), whole((ROWS, HEAD))],
        prompt_len, own, other, sensitivity,
        flops=2 * 2 * ROWS * HALF * HEAD, moved=6 << 20, megabytes=24,
        grid=(1,),
        out_specs=(whole((SHARE, HALF)),) * 4,
        scratch_shapes=[pltpu.VMEM((HEAD, 512), F32)],
    )
    height = HEAD + EXTRA
    packed, one, two, three = local(
        pack_kernel,
        (shape((NEAR, height, HEAD), BF16),) + (shape((SHARE, HALF), BF16),) * 3,
        [VMEM] * 2 + [ANY] * 3,
        value_weight, parts, one, two, three,
        moved=600 << 10,
        out_specs=(VMEM, ANY, ANY, ANY),
        input_output_aliases={2: 1, 3: 2, 4: 3},
    )
    near = lax.all_to_all(packed.reshape(-1, HEAD), ("yq", "z"), 0, 0, tiled=True).reshape(NEAR, height, HEAD)
    outside = [(y, (y + 1) % 8 if y % 2 else (y - 1) % 8) for y in range(8)]
    far = lax.ppermute(near, ("yh", "yp", "yq"), outside)

    sent = [
        lax.ppermute(chunk, "x", [(i, (i + step) % XS) for i in range(XS)])
        for step, chunk in ((1, one), (2, two), (3, three))
    ]
    summed = local(
        add_kernel,
        shape((BLOCKS, SHARE, HEAD), BF16),
        [tile, whole((SHARE, HALF))] + [whole((SHARE, HALF))] * 3,
        near, keep, *sent,
        moved=2 << 20,
        grid=(1,),
        out_specs=whole((BLOCKS, SHARE, HEAD)),
    )
    terms = lax.all_to_all(summed.reshape(-1, HEAD), ("yp", "yq", "z"), 0, 0, tiled=True)

    mine, theirs = local(
        project_kernel,
        (shape((ROWS, HEAD), F32),) * 2,
        [VMEM] * 4,
        near, far, own, other,
        flops=2 * 2 * ROWS * HALF * HEAD, moved=6 << 20, megabytes=24,
    )
    projected = (mine + lax.ppermute(theirs, "c", SWAP)).astype(BF16)

    high = SHARE + 8
    joined = local(
        join_kernel,
        shape((2 * XS, high, HEAD), F32),
        [whole((BLOCKS, SHARE, HEAD)), tile, tile],
        terms.reshape(BLOCKS, SHARE, HEAD), near, far,
        moved=1 << 20,
        grid=(1,),
        out_specs=whole((2 * XS, high, HEAD)),
    )
    shares = lax.all_to_all(joined.reshape(-1, HEAD), DP, 0, 0, tiled=True).reshape(2 * XS, high, HEAD)
    weight_grad, margins, loss = local(
        last_kernel,
        (shape((HEAD, HEAD), F32), shape((1, PAIRS), F32), shape((1, 1), F32)),
        [VMEM],
        shares,
        moved=300 << 10,
        out_specs=(VMEM, VMEM, SMEM),
    )
    return projected, weight_grad, margins.reshape(PAIRS), loss.reshape(())


def solution(mesh):
    devices = mesh.devices.reshape(tuple(size for _, size in SIZES))
    return jax.shard_map(
        body,
        mesh=Mesh(devices, NAMES),
        in_specs=(
            P(DP + FSDP, None),
            P(FSDP, None),
            P(DP + FSDP, None),
            P(DP + FSDP),
            P(DP + FSDP),
            P(),
        ),
        out_specs=(P(DP + FSDP, None), P(FSDP, None), P(), P()),
        check_vma=False,
    )
```
